32 devices in a mesh: groups: 1, row: 4 (over x, core), col: 8 (over z, y).
Axes of the slice: x: 2, y: 2, z: 4, core: 2. Of those that a mesh axis runs over, the one named last changes fastest.
Arguments:
- a_tiles: bfloat16 [128, 27, 128, 128], P(('groups', 'row', 'col')), may hold values from -0.5 to 0.5
- a_cols: int32 [128, 27], P(('groups', 'row', 'col')), may hold values from 0 to 127, as said below
- p_tiles: bfloat16 [128, 4, 128, 128], P(('groups', 'row', 'col')), may hold values from -0.5 to 0.5
- p_cols: int32 [128, 4], P('groups'), may hold values from 0 to 15, as said below
Outputs:
- coarse: float32 [2048, 1536], P(('groups', 'row', 'col'))
The draws below stay inside these ranges and needn't reach their ends.
Inputs may be any that keep to these rules, and one draw needn't show every extreme that they name: `a_cols`: in each row i the 27 columns are distinct, include i itself, and each equals (i + d) mod 128 for some d with |d| <= 16. `p_cols`: in each row i the 4 columns are distinct, include the row's aggregate (i // 32) * 4 + (i % 32) // 8, and all lie in the coarse blocks of the row's own grid row, (i // 32) * 4 to (i // 32) * 4 + 3.
All inputs are finite; a program needn't handle non-finite values.
Results may differ from the reference program's by a relative error of at most 0.008.
Values may be sent and summed in bfloat16 or wider, within the bound.
A program may use at most 128 MiB of HBM per device.

```python
import jax
import jax.numpy as jnp
from jax import lax

B = 128
KA = 27
KP = 4
AGG = 8
FBR = 32
H = 16
FB = 128
CBR = 4
CB = 16
W = 12
N_ROW = 4


def draw_a_cols(key, part):
    key = jax.random.fold_in(key, 11)
    width_span = 2 * H
    rank_scores = jax.random.randint(key, (FB, width_span), 0, 65536) * width_span + jnp.arange(width_span, dtype=jnp.int32)
    picked_idx = jnp.argsort(rank_scores, axis=1)[:, :KA - 1].astype(jnp.int32)
    offsets = jnp.where(picked_idx < H, picked_idx - H, picked_idx - H + 1)
    offsets = jnp.concatenate([jnp.zeros((FB, 1), jnp.int32), offsets], axis=1)
    row_ids = jnp.arange(FB, dtype=jnp.int32)[:, None]
    return ((row_ids + offsets) % FB).astype(jnp.int32)


def draw_p_cols(key, part):
    key = jax.random.fold_in(key, 23)
    row_ids = jnp.arange(FB, dtype=jnp.int32)
    slab_ids = row_ids // FBR
    group_ids = row_ids % FBR // AGG
    choices_count = CBR - 1
    rank_scores = jax.random.randint(key, (FB, choices_count), 0, 65536) * choices_count + jnp.arange(choices_count, dtype=jnp.int32)
    picked_idx = jnp.argsort(rank_scores, axis=1)[:, :KP - 1].astype(jnp.int32)
    others = (group_ids[:, None] + 1 + picked_idx) % CBR
    local_cols = jnp.concatenate([group_ids[:, None], others], axis=1)
    return (slab_ids[:, None] * CBR + local_cols).astype(jnp.int32)


def level_of(own_key, dims, shards, least, largest):
    level, own = 1.0, jax.random.fold_in(own_key, 6)
    for position, shards_of in shards:
        heights = jnp.exp(jax.random.uniform(jax.random.fold_in(own, position), (shards_of,), jnp.float32, least / len(shards), largest / len(shards)))
        level = level * jnp.repeat(heights, dims[position] // shards_of).reshape([-1 if axis == position else 1 for axis in range(len(dims))])
    return level


def bell_draw(stream_key, dims, scale, most, split=(), held_as=jnp.bfloat16):
    factor_of = level_of(stream_key, dims, split, -0.22, 0.18) if split else 1.0
    entries = jax.random.normal(stream_key, dims, jnp.float32) * scale * factor_of
    return jnp.minimum(jnp.maximum(entries, -most), most).astype(held_as)


def setup_inputs(seed: int = 0, part: int = 0) -> dict:
    key_of = jax.random.split(jax.random.key(seed), 5)
    own_keys = jax.random.split(jax.random.fold_in(key_of[4], part), 5)
    a_tiles = bell_draw(own_keys[0], (FB, KA, B, B), B ** -0.5, 0.5, ((0, 32),))
    a_cols = draw_a_cols(jax.random.fold_in(jax.random.fold_in(key_of[4], part), 71), part)
    p_tiles = bell_draw(own_keys[2], (FB, KP, B, B), B ** -0.5, 0.5, ((0, 32),))
    p_cols = draw_p_cols(jax.random.fold_in(jax.random.fold_in(key_of[4], part), 71), part)
    return {"a_tiles": a_tiles, "a_cols": a_cols, "p_tiles": p_tiles, "p_cols": p_cols}


def reference(a_tiles, a_cols, p_tiles, p_cols):
    window_ids = jnp.arange(W, dtype=jnp.int32)
    owner_ids = jnp.arange(CBR, dtype=jnp.int32)
    highest = lax.Precision.HIGHEST

    def add_row(coarse_sum, row_items):
        row_id, a_row_tiles, col_ids, p_row_tiles, p_row_cols = row_items
        slab_id = row_id // FBR
        picked = jnp.take(p_tiles, col_ids, axis=0)
        picked_cols = jnp.take(p_cols, col_ids, axis=0)
        band_index = (col_ids // FBR - slab_id + 1) % N_ROW
        window_pos = band_index[:, None] * CBR + picked_cols % CBR
        products = jnp.einsum('jab,jqbc->jqac', a_row_tiles.astype(jnp.float32), picked.astype(jnp.float32), precision=highest)
        window_marks = (window_pos[:, :, None] == window_ids).astype(jnp.float32)
        merged = jnp.einsum('jqw,jqac->awc', window_marks, products, precision=highest)
        ap_row = merged.reshape(B, W * B).astype(jnp.bfloat16)
        spread = jnp.einsum('qba,bn->qan', p_row_tiles.astype(jnp.float32), ap_row.astype(jnp.float32), precision=highest)
        owner_marks = ((p_row_cols % CBR)[:, None] == owner_ids).astype(jnp.float32)
        contrib = jnp.einsum('qi,qan->ian', owner_marks, spread, precision=highest).reshape(CBR * B, W * B)
        current = lax.dynamic_index_in_dim(coarse_sum, slab_id, 0, keepdims=False)
        coarse_sum = lax.dynamic_update_index_in_dim(coarse_sum, current + contrib, slab_id, 0)
        return coarse_sum, None

    start_sum = jnp.zeros((N_ROW, CBR * B, W * B), jnp.float32)
    row_numbers = jnp.arange(FB, dtype=jnp.int32)
    total_sum, _ = lax.scan(add_row, start_sum, (row_numbers, a_tiles, a_cols, p_tiles, p_cols))
    return total_sum.reshape(CB * B, W * B)
```

```python
import functools

import jax
import jax.numpy as jnp
from jax import lax
from jax.experimental import pallas as pl
from jax.experimental.pallas import tpu as pltpu
from jax.sharding import PartitionSpec as P

AGG = 8
MESH = pl.DeviceIdType.MESH


def kernel(dims, slots, a_hbm, p_hbm, out, a_scr, p_scr, ad, pt, rowbuf, halo, acc, partf, part16, yrecv, zsend, own,
           zrecv, loc_sem, ag_send, ag_recv, h_send, h_recv, y_send, y_recv, z_send, z_recv):
    R, C, Z, Y, D, KA, KP, B, CBR = dims
    NB = CBR * B
    reach = C // 2
    half = C - reach
    r, c = lax.axis_index("row"), lax.axis_index("col")
    z, y = c // Y, c % Y
    low = c < half
    r_up, r_down = lax.rem(r + 1, R), lax.rem(r + R - 1, R)

    def dev(row, col):
        return {"row": row, "col": col}

    copy_p = pltpu.make_async_copy(p_hbm, p_scr.at[:, pl.ds(0, KP)], loc_sem.at[0])
    copy_a = pltpu.make_async_copy(a_hbm, a_scr.at[:, pl.ds(0, KA)], loc_sem.at[1])
    copy_p.start()
    copy_a.start()
    barrier = pltpu.get_barrier_semaphore()
    for k in range(1, Z):
        pl.semaphore_signal(barrier, inc=1, device_id=dev(r, lax.rem(z + k, Z) * Y + y), device_id_type=MESH)
    if Y == 2:
        pl.semaphore_signal(barrier, inc=1, device_id=dev(r, z * Y + 1 - y), device_id_type=MESH)
    pl.semaphore_signal(barrier, inc=1, device_id=dev(r_up, c), device_id_type=MESH)
    pl.semaphore_signal(barrier, inc=1, device_id=dev(r_down, c), device_id_type=MESH)

    for i in range(D):
        p_scr[i, KP] = jnp.zeros((B, B), jnp.bfloat16)
        a_scr[i, KA] = jnp.zeros((B, B), jnp.bfloat16)
    copy_p.wait()
    for i in range(D):
        for m in range(CBR):
            rowbuf[c, i * B:(i + 1) * B, m * B:(m + 1) * B] = p_scr[i, slots[i, m]]
    pl.semaphore_wait(barrier, Z - 1 + (Y - 1) + 2)

    def ag_copy(kind, slab, col):
        return pltpu.make_async_remote_copy(
            src_ref=rowbuf.at[slab], dst_ref=rowbuf.at[slab], send_sem=ag_send.at[kind, slab],
            recv_sem=ag_recv.at[slab], device_id=dev(r, col), device_id_type=MESH)

    def halo_copy(slab, idx, row):
        return pltpu.make_async_remote_copy(
            src_ref=rowbuf.at[slab], dst_ref=halo.at[idx], send_sem=h_send.at[idx],
            recv_sem=h_recv.at[idx], device_id=dev(row, c), device_id_type=MESH)

    def halo_forward(slab):
        @pl.when(jnp.logical_and(low, slab >= c + half))
        def _():
            halo_copy(slab, slab - half, r_up).start()

        @pl.when(jnp.logical_and(jnp.logical_not(low), slab <= c - reach))
        def _():
            halo_copy(slab, slab, r_down).start()

    def use(buf, slab, d, band):
        for n in range(0, NB, 256):
            acc[band, :, n:n + 256] += jnp.dot(ad[d + reach], buf[slab, :, n:n + 256],
                                               preferred_element_type=jnp.float32)

    def use_row(slab):
        d = slab - c

        @pl.when(jnp.logical_and(d <= reach, d >= -reach))
        def _():
            use(rowbuf, slab, d, 0)

    @pl.when(z + 1 < Z)
    def _():
        ag_copy(0, c, c + Y).start()

    @pl.when(z > 0)
    def _():
        ag_copy(1, c, c - Y).start()

    if Y == 2:
        ag_copy(2, c, z * Y + 1 - y).start()

    acc[...] = jnp.zeros_like(acc)
    copy_a.wait()

    def build(d, carry):
        for i in range(D):
            for s in range(D):
                ad[d, i * B:(i + 1) * B, s * B:(s + 1) * B] = a_scr[i, slots[i, CBR + d * D + s]]
        return carry

    lax.fori_loop(0, 2 * reach + 1, build, 0)
    pt[...] = rowbuf[c].T
    use(rowbuf, c, 0, 0)

    def line(k, carry):
        below, above = z - k, z + k
        for there, ok in ((below, below >= 0), (above, above < Z)):
            slab = there * Y + y

            @pl.when(ok)
            def _():
                ag_copy(0, slab, c).wait_recv()
                if there is below:
                    @pl.when(z + 1 < Z)
                    def _():
                        ag_copy(0, slab, c + Y).start()
                else:
                    @pl.when(z > 0)
                    def _():
                        ag_copy(1, slab, c - Y).start()
                if Y == 2:
                    ag_copy(2, slab, z * Y + 1 - y).start()
                halo_forward(slab)
        for there, ok in ((below, below >= 0), (above, above < Z)):
            @pl.when(ok)
            def _():
                use_row(there * Y + y)
        if Y == 2:
            for there, ok in ((z - k + 1, z - k + 1 >= 0), (z + k - 1, jnp.logical_and(z + k - 1 < Z, k > 1))):
                @pl.when(ok)
                def _():
                    slab = there * Y + 1 - y
                    ag_copy(2, slab, c).wait_recv()
                    halo_forward(slab)
                    use_row(slab)
        return carry

    lax.fori_loop(1, Z + Y - 1, line, 0)

    def y_copy(band):
        return pltpu.make_async_remote_copy(
            src_ref=part16.at[band], dst_ref=yrecv.at[band], send_sem=y_send.at[band],
            recv_sem=y_recv.at[band], device_id=dev(r, z * Y + 1 - y), device_id_type=MESH)

    share = NB // C

    def partial(band):
        for n in range(0, NB, 256):
            ap = acc[band, :, n:n + 256].astype(jnp.bfloat16)
            res = jnp.dot(pt[...], ap, preferred_element_type=jnp.float32)
            for t in range(C):
                partf[band, t % Y, t // Y, :, n:n + 256] = res[t * share:(t + 1) * share]
        if Y == 2:
            part16[band] = partf[band, 1 - y].astype(jnp.bfloat16)
            y_copy(band).start()

    partial(0)

    def halo_use(t, carry):
        idx = jnp.where(low, t, reach - 1 - t)

        @pl.when(jnp.logical_or(jnp.logical_and(low, idx >= c), jnp.logical_and(jnp.logical_not(low), idx <= c - reach)))
        def _():
            halo_copy(c, idx, r_up).wait_recv()
            use(halo, idx, jnp.where(low, idx - reach - c, C + idx - c), 1)
        return carry

    lax.fori_loop(0, reach, halo_use, 0)
    partial(1)

    def z_copy(band, to, slot):
        return pltpu.make_async_remote_copy(
            src_ref=zsend.at[band, to], dst_ref=zrecv.at[band, slot], send_sem=z_send.at[band, to],
            recv_sem=z_recv.at[band, slot], device_id=dev(r, to * Y + y), device_id_type=MESH)

    for band in range(2):
        if Y == 2:
            y_copy(band).wait_recv()
            own[band] = partf[band, y, z] + yrecv[band, z].astype(jnp.float32)
        else:
            own[band] = partf[band, y, z]
        for t in range(Z):
            @pl.when(t != z)
            def _():
                total = partf[band, y, t]
                if Y == 2:
                    total = total + yrecv[band, t].astype(jnp.float32)
                zsend[band, t] = total.astype(jnp.bfloat16)
                z_copy(band, t, z).start()

    out[...] = jnp.zeros_like(out)
    out[:, NB:2 * NB] = own[0]

    @pl.when(low)
    def _():
        out[:, 0:NB] = own[1]

    @pl.when(jnp.logical_not(low))
    def _():
        out[:, 2 * NB:3 * NB] = own[1]

    for band in range(2):
        for t in range(Z):
            start = NB if band == 0 else (0 if t < Z // 2 else 2 * NB)

            @pl.when(t != z)
            def _():
                z_copy(band, t, t).wait_recv()
                out[:, start:start + NB] += zrecv[band, t].astype(jnp.float32)

    for band in range(2):
        if Y == 2:
            y_copy(band).wait_send()
        for t in range(Z):
            @pl.when(t != z)
            def _():
                z_copy(band, t, z).wait_send()

    def drain(slab, carry):
        mine = slab % Y == y
        there = slab // Y

        @pl.when(jnp.logical_and(mine, jnp.logical_and(there <= z, z + 1 < Z)))
        def _():
            ag_copy(0, slab, c).wait_send()

        @pl.when(jnp.logical_and(mine, jnp.logical_and(there >= z, z > 0)))
        def _():
            ag_copy(1, slab, c).wait_send()

        if Y == 2:
            @pl.when(mine)
            def _():
                ag_copy(2, slab, c).wait_send()

        @pl.when(jnp.logical_and(low, slab >= c + half))
        def _():
            halo_copy(slab, slab - half, r_up).wait_send()

        @pl.when(jnp.logical_and(jnp.logical_not(low), slab <= c - reach))
        def _():
            halo_copy(slab, slab, r_down).wait_send()
        return carry

    lax.fori_loop(0, C, drain, 0)


def local(Y, a_tiles, a_cols, p_tiles, p_cols):
    D, KA, B = a_tiles.shape[:3]
    KP = p_tiles.shape[1]
    C, R = lax.axis_size("col"), lax.axis_size("row")
    Z = C // Y
    slab_len = D * C
    total_rows = slab_len * R
    CBR = slab_len // AGG
    NB = CBR * B
    reach = slab_len // 2
    rs = C // 2
    first_row = (lax.axis_index("row") * C + lax.axis_index("col")) * D
    own_cols = lax.dynamic_slice_in_dim(p_cols, first_row, D, 0) % CBR
    m_ids = jnp.arange(CBR, dtype=jnp.int32)
    q_ids = KP - jnp.arange(KP, dtype=jnp.int32)
    p_slot = KP - jnp.sum(jnp.where(own_cols[:, :, None] == m_ids, q_ids[:, None], 0), axis=1)
    rel = (a_cols - first_row + reach) % total_rows
    e_ids = jnp.arange(2 * reach + D, dtype=jnp.int32)
    j_ids = KA - jnp.arange(KA, dtype=jnp.int32)
    a_slot = KA - jnp.sum(jnp.where(rel[:, :, None] == e_ids, j_ids[:, None], 0), axis=1)
    slots = jnp.concatenate([p_slot, a_slot], axis=1)
    bf, f32 = jnp.bfloat16, jnp.float32
    share = NB // C
    S = pltpu.SemaphoreType.DMA
    V = pltpu.VMEM
    return pl.pallas_call(
        functools.partial(kernel, (R, C, Z, Y, D, KA, KP, B, CBR)),
        out_shape=jax.ShapeDtypeStruct((share, 3 * NB), f32),
        in_specs=[pl.BlockSpec(memory_space=pltpu.SMEM), pl.BlockSpec(memory_space=pl.ANY),
                  pl.BlockSpec(memory_space=pl.ANY)],
        out_specs=pl.BlockSpec(memory_space=pltpu.VMEM),
        scratch_shapes=[
            V((D, KA + 1, B, B), bf), V((D, KP + 1, B, B), bf),
            V((2 * rs + 1, D * B, D * B), bf), V((NB, D * B), bf),
            V((C, D * B, NB), bf), V((rs, D * B, NB), bf),
            V((2, D * B, NB), f32), V((2, Y, Z, share, NB), f32),
            V((2, Z, share, NB), bf), V((2, Z, share, NB), bf),
            V((2, Z, share, NB), bf), V((2, share, NB), f32), V((2, Z, share, NB), bf),
            S((2,)), S((3, C)), S((C,)), S((rs,)), S((rs,)), S((2,)), S((2,)), S((2, Z)), S((2, Z)),
        ],
        compiler_params=pltpu.CompilerParams(collective_id=0, has_side_effects=True,
                                             vmem_limit_bytes=60 * 1024 * 1024),
    )(slots, a_tiles, p_tiles)


def solution(mesh):
    Y = 2 if mesh.shape["groups"] == 1 else 1
    in_specs = (
        P(("groups", "row", "col"), None, None, None),
        P(("groups", "row", "col"), None),
        P(("groups", "row", "col"), None, None, None),
        P("groups", None),
    )
    out_specs = P(("groups", "row", "col"), None)
    return jax.shard_map(functools.partial(local, Y), mesh=mesh, in_specs=in_specs, out_specs=out_specs,
                         check_vma=False)
```

```python
import functools

import jax
import jax.numpy as jnp
from jax import lax
from jax.experimental import pallas as pl
from jax.experimental.pallas import tpu as pltpu
from jax.sharding import PartitionSpec as P

AGG = 8
MESH = pl.DeviceIdType.MESH


def kernel(dims, slots, a_hbm, p_hbm, out, a_scr, p_scr, ad, pt, rowbuf, halo, acc, partf, part16, yrecv, zsend, own,
           zrecv, loc_sem, ag_send, ag_recv, h_send, h_recv, y_send, y_recv, z_send, z_recv):
    R, C, Z, Y, D, KA, KP, B, CBR = dims
    NB = CBR * B
    reach = C // 2
    half = C - reach
    r, c = lax.axis_index("row"), lax.axis_index("col")
    z, y = c // Y, c % Y
    low = c < half
    r_up, r_down = lax.rem(r + 1, R), lax.rem(r + R - 1, R)

    def dev(row, col):
        return {"row": row, "col": col}

    copy_p = pltpu.make_async_copy(p_hbm, p_scr.at[:, pl.ds(0, KP)], loc_sem.at[0])
    copy_a = pltpu.make_async_copy(a_hbm, a_scr.at[:, pl.ds(0, KA)], loc_sem.at[1])
    copy_p.start()
    copy_a.start()
    barrier = pltpu.get_barrier_semaphore()
    for k in range(1, Z):
        pl.semaphore_signal(barrier, inc=1, device_id=dev(r, lax.rem(z + k, Z) * Y + y), device_id_type=MESH)
    if Y == 2:
        pl.semaphore_signal(barrier, inc=1, device_id=dev(r, z * Y + 1 - y), device_id_type=MESH)
    pl.semaphore_signal(barrier, inc=1, device_id=dev(r_up, c), device_id_type=MESH)
    pl.semaphore_signal(barrier, inc=1, device_id=dev(r_down, c), device_id_type=MESH)

    for i in range(D):
        p_scr[i, KP] = jnp.zeros((B, B), jnp.bfloat16)
        a_scr[i, KA] = jnp.zeros((B, B), jnp.bfloat16)
    copy_p.wait()
    for i in range(D):
        for m in range(CBR):
            rowbuf[c, i * B:(i + 1) * B, m * B:(m + 1) * B] = p_scr[i, slots[i, m]]
    pl.semaphore_wait(barrier, Z - 1 + (Y - 1) + 2)

    H = 2
    hb = D * B // H

    def piece(h):
        return pl.ds(pl.multiple_of(h * hb, hb), hb)

    def ag_copy(kind, slab, h, col):
        return pltpu.make_async_remote_copy(
            src_ref=rowbuf.at[slab, piece(h)], dst_ref=rowbuf.at[slab, piece(h)], send_sem=ag_send.at[kind, slab, h],
            recv_sem=ag_recv.at[slab, h], device_id=dev(r, col), device_id_type=MESH)

    def halo_copy(slab, idx, h, row):
        return pltpu.make_async_remote_copy(
            src_ref=rowbuf.at[slab, piece(h)], dst_ref=halo.at[idx, piece(h)], send_sem=h_send.at[idx, h],
            recv_sem=h_recv.at[idx, h], device_id=dev(row, c), device_id_type=MESH)

    def when(*conds):
        return pl.when(functools.reduce(jnp.logical_and, conds))

    def up_ok(slab, h):
        mine, there = slab % Y == y, slab // Y
        by_line = jnp.logical_or(mine, there == 0) if h == H - 1 else mine
        return functools.reduce(jnp.logical_and, (by_line, there <= z, z + 1 < Z))

    def down_ok(slab, h):
        mine, there = slab % Y == y, slab // Y
        by_line = jnp.logical_or(mine, there == Z - 1) if h == H - 1 else mine
        return functools.reduce(jnp.logical_and, (by_line, there >= z, z > 0))

    def y_ok(slab, h):
        mine, there = slab % Y == y, slab // Y
        if h == H - 1:
            inner = jnp.logical_and(there > 0, there < Z - 1)
            return jnp.logical_and(mine, jnp.logical_or(slab == c, inner))
        return mine

    def halo_up(slab):
        return jnp.logical_and(low, slab >= c + half)

    def halo_down(slab):
        return jnp.logical_and(jnp.logical_not(low), slab <= c - reach)

    def each(slab, h, act):
        @pl.when(up_ok(slab, h))
        def _():
            act(ag_copy(0, slab, h, c + Y))

        @pl.when(down_ok(slab, h))
        def _():
            act(ag_copy(1, slab, h, c - Y))

        if Y == 2:
            @pl.when(y_ok(slab, h))
            def _():
                act(ag_copy(2, slab, h, z * Y + 1 - y))

        @pl.when(halo_up(slab))
        def _():
            act(halo_copy(slab, slab - half, h, r_up))

        @pl.when(halo_down(slab))
        def _():
            act(halo_copy(slab, slab, h, r_down))

    def start(copy):
        copy.start()

    def receive(slab, h):
        ag_copy(0, slab, h, c).wait_recv()
        each(slab, h, start)

    def use(buf, slab, d, band):
        for n in range(0, NB, 256):
            acc[band, :, n:n + 256] += jnp.dot(ad[d + reach], buf[slab, :, n:n + 256],
                                               preferred_element_type=jnp.float32)

    def use_row(slab):
        d = slab - c

        @pl.when(jnp.logical_and(d <= reach, d >= -reach))
        def _():
            use(rowbuf, slab, d, 0)

    for h in range(H):
        each(c, h, start)

    acc[...] = jnp.zeros_like(acc)
    copy_a.wait()

    def build(d, carry):
        for i in range(D):
            for s in range(D):
                ad[d, i * B:(i + 1) * B, s * B:(s + 1) * B] = a_scr[i, slots[i, CBR + d * D + s]]
        return carry

    lax.fori_loop(0, 2 * reach + 1, build, 0)
    pt[...] = rowbuf[c].T
    use(rowbuf, c, 0, 0)

    def y_copy(band):
        return pltpu.make_async_remote_copy(
            src_ref=part16.at[band], dst_ref=yrecv.at[band], send_sem=y_send.at[band],
            recv_sem=y_recv.at[band], device_id=dev(r, z * Y + 1 - y), device_id_type=MESH)

    share = NB // C

    def partial(band):
        for n in range(0, NB, 256):
            ap = acc[band, :, n:n + 256].astype(jnp.bfloat16)
            res = jnp.dot(pt[...], ap, preferred_element_type=jnp.float32)
            for t in range(C):
                partf[band, t % Y, t // Y, :, n:n + 256] = res[t * share:(t + 1) * share]
        if Y == 2:
            part16[band] = partf[band, 1 - y].astype(jnp.bfloat16)
            y_copy(band).start()

    def line(k, carry):
        pairs = ((z - k, z - k >= 0), (z + k, z + k < Z))
        cross = ((z - k + 1, z - k + 1 >= 0), (z + k - 1, jnp.logical_and(z + k - 1 < Z, k > 1)))
        for h in range(H):
            for there, ok in pairs:
                @pl.when(ok)
                def _():
                    receive(there * Y + y, h)
            if Y == 2:
                for there, ok in cross:
                    @pl.when(ok)
                    def _():
                        receive(there * Y + 1 - y, h)
        for there, ok in pairs:
            @pl.when(ok)
            def _():
                use_row(there * Y + y)
        if Y == 2:
            for there, ok in cross:
                @pl.when(ok)
                def _():
                    use_row(there * Y + 1 - y)

        @pl.when(k == Z // 2 + Y - 1)
        def _():
            partial(0)
        return carry

    lax.fori_loop(1, Z + Y - 1, line, 0)

    def halo_use(t, carry):
        idx = jnp.where(low, t, reach - 1 - t)

        @pl.when(jnp.logical_or(jnp.logical_and(low, idx >= c), jnp.logical_and(jnp.logical_not(low), idx <= c - reach)))
        def _():
            for h in range(H):
                halo_copy(c, idx, h, r_up).wait_recv()
            use(halo, idx, jnp.where(low, idx - reach - c, C + idx - c), 1)
        return carry

    lax.fori_loop(0, reach, halo_use, 0)
    partial(1)

    def z_copy(band, to, slot):
        return pltpu.make_async_remote_copy(
            src_ref=zsend.at[band, to], dst_ref=zrecv.at[band, slot], send_sem=z_send.at[band, to],
            recv_sem=z_recv.at[band, slot], device_id=dev(r, to * Y + y), device_id_type=MESH)

    for band in range(2):
        if Y == 2:
            y_copy(band).wait_recv()
            own[band] = partf[band, y, z] + yrecv[band, z].astype(jnp.float32)
        else:
            own[band] = partf[band, y, z]
        for t in range(Z):
            @pl.when(t != z)
            def _():
                total = partf[band, y, t]
                if Y == 2:
                    total = total + yrecv[band, t].astype(jnp.float32)
                zsend[band, t] = total.astype(jnp.bfloat16)
                z_copy(band, t, z).start()

    out[...] = jnp.zeros_like(out)
    out[:, NB:2 * NB] = own[0]

    @pl.when(low)
    def _():
        out[:, 0:NB] = own[1]

    @pl.when(jnp.logical_not(low))
    def _():
        out[:, 2 * NB:3 * NB] = own[1]

    for band in range(2):
        for t in range(Z):
            start = NB if band == 0 else (0 if t < Z // 2 else 2 * NB)

            @pl.when(t != z)
            def _():
                z_copy(band, t, t).wait_recv()
                out[:, start:start + NB] += zrecv[band, t].astype(jnp.float32)

    for band in range(2):
        if Y == 2:
            y_copy(band).wait_send()
        for t in range(Z):
            @pl.when(t != z)
            def _():
                z_copy(band, t, z).wait_send()

    def drain(slab, carry):
        for h in range(H):
            each(slab, h, lambda copy: copy.wait_send())
        return carry

    lax.fori_loop(0, C, drain, 0)


def local(Y, a_tiles, a_cols, p_tiles, p_cols):
    D, KA, B = a_tiles.shape[:3]
    KP = p_tiles.shape[1]
    C, R = lax.axis_size("col"), lax.axis_size("row")
    Z = C // Y
    slab_len = D * C
    total_rows = slab_len * R
    CBR = slab_len // AGG
    NB = CBR * B
    reach = slab_len // 2
    rs = C // 2
    first_row = (lax.axis_index("row") * C + lax.axis_index("col")) * D
    own_cols = lax.dynamic_slice_in_dim(p_cols, first_row, D, 0) % CBR
    m_ids = jnp.arange(CBR, dtype=jnp.int32)
    q_ids = KP - jnp.arange(KP, dtype=jnp.int32)
    p_slot = KP - jnp.max(jnp.where(own_cols[:, :, None] == m_ids, q_ids[:, None], 0), axis=1)
    rel = (a_cols - first_row + reach) % total_rows
    e_ids = jnp.arange(2 * reach + D, dtype=jnp.int32)
    j_ids = KA - jnp.arange(KA, dtype=jnp.int32)
    a_slot = KA - jnp.max(jnp.where(rel[:, :, None] == e_ids, j_ids[:, None], 0), axis=1)
    slots = jnp.concatenate([p_slot, a_slot], axis=1)
    bf, f32 = jnp.bfloat16, jnp.float32
    share = NB // C
    S = pltpu.SemaphoreType.DMA
    V = pltpu.VMEM
    return pl.pallas_call(
        functools.partial(kernel, (R, C, Z, Y, D, KA, KP, B, CBR)),
        out_shape=jax.ShapeDtypeStruct((share, 3 * NB), f32),
        in_specs=[pl.BlockSpec(memory_space=pltpu.SMEM), pl.BlockSpec(memory_space=pl.ANY),
                  pl.BlockSpec(memory_space=pl.ANY)],
        out_specs=pl.BlockSpec(memory_space=pltpu.VMEM),
        scratch_shapes=[
            V((D, KA + 1, B, B), bf), V((D, KP + 1, B, B), bf),
            V((2 * rs + 1, D * B, D * B), bf), V((NB, D * B), bf),
            V((C, D * B, NB), bf), V((rs, D * B, NB), bf),
            V((2, D * B, NB), f32), V((2, Y, Z, share, NB), f32),
            V((2, Z, share, NB), bf), V((2, Z, share, NB), bf),
            V((2, Z, share, NB), bf), V((2, share, NB), f32), V((2, Z, share, NB), bf),
            S((2,)), S((3, C, 2)), S((C, 2)), S((rs, 2)), S((rs, 2)), S((2,)), S((2,)), S((2, Z)), S((2, Z)),
        ],
        compiler_params=pltpu.CompilerParams(collective_id=0, has_side_effects=True,
                                             vmem_limit_bytes=60 * 1024 * 1024),
    )(slots, a_tiles, p_tiles)


def solution(mesh):
    Y = 2 if mesh.shape["groups"] == 1 else 1
    in_specs = (
        P(("groups", "row", "col"), None, None, None),
        P(("groups", "row", "col"), None),
        P(("groups", "row", "col"), None, None, None),
        P("groups", None),
    )
    out_specs = P(("groups", "row", "col"), None)
    return jax.shard_map(functools.partial(local, Y), mesh=mesh, in_specs=in_specs, out_specs=out_specs,
                         check_vma=False)
```

```python
import functools

import jax
import jax.numpy as jnp
from jax import lax
from jax.experimental import pallas as pl
from jax.experimental.pallas import tpu as pltpu
from jax.sharding import PartitionSpec as P

AGG = 8
MESH = pl.DeviceIdType.MESH


def kernel(dims, slots, a_hbm, p_hbm, out, a_scr, p_scr, ad, pt, rowbuf, halo, acc, partf, part16, yrecv, zsend, own,
           zrecv, loc_sem, ag_send, ag_recv, h_send, h_recv, y_send, y_recv, z_send, z_recv):
    R, C, Z, Y, D, KA, KP, B, CBR = dims
    NB = CBR * B
    reach = C // 2
    half = C - reach
    r, c = lax.axis_index("row"), lax.axis_index("col")
    z, y = c // Y, c % Y
    low = c < half
    r_up, r_down = lax.rem(r + 1, R), lax.rem(r + R - 1, R)

    def dev(row, col):
        return {"row": row, "col": col}

    copy_p = pltpu.make_async_copy(p_hbm, p_scr.at[:, pl.ds(0, KP)], loc_sem.at[0])
    copy_a = pltpu.make_async_copy(a_hbm, a_scr.at[:, pl.ds(0, KA)], loc_sem.at[1])
    copy_p.start()
    copy_a.start()
    barrier = pltpu.get_barrier_semaphore()
    for k in range(1, Z):
        pl.semaphore_signal(barrier, inc=1, device_id=dev(r, lax.rem(z + k, Z) * Y + y), device_id_type=MESH)
    if Y == 2:
        pl.semaphore_signal(barrier, inc=1, device_id=dev(r, z * Y + 1 - y), device_id_type=MESH)
    pl.semaphore_signal(barrier, inc=1, device_id=dev(r_up, c), device_id_type=MESH)
    pl.semaphore_signal(barrier, inc=1, device_id=dev(r_down, c), device_id_type=MESH)

    for i in range(D):
        p_scr[i, KP] = jnp.zeros((B, B), jnp.bfloat16)
        a_scr[i, KA] = jnp.zeros((B, B), jnp.bfloat16)
    copy_p.wait()
    for i in range(D):
        for m in range(CBR):
            rowbuf[c, i * B:(i + 1) * B, m * B:(m + 1) * B] = p_scr[i, slots[i, m]]
    pl.semaphore_wait(barrier, Z - 1 + (Y - 1) + 2)

    H = 4
    hb = D * B // H

    def piece(h):
        return pl.ds(pl.multiple_of(h * hb, hb), hb)

    def ag_copy(kind, slab, h, col):
        return pltpu.make_async_remote_copy(
            src_ref=rowbuf.at[slab, piece(h)], dst_ref=rowbuf.at[slab, piece(h)], send_sem=ag_send.at[kind, slab, h],
            recv_sem=ag_recv.at[slab, h], device_id=dev(r, col), device_id_type=MESH)

    def halo_copy(slab, idx, h, row):
        return pltpu.make_async_remote_copy(
            src_ref=rowbuf.at[slab, piece(h)], dst_ref=halo.at[idx, piece(h)], send_sem=h_send.at[idx, h],
            recv_sem=h_recv.at[idx, h], device_id=dev(row, c), device_id_type=MESH)

    def when(*conds):
        return pl.when(functools.reduce(jnp.logical_and, conds))

    def up_ok(slab, h):
        mine, there = slab % Y == y, slab // Y
        by_line = jnp.logical_or(mine, there == 0) if h >= H // 2 else mine
        return functools.reduce(jnp.logical_and, (by_line, there <= z, z + 1 < Z))

    def down_ok(slab, h):
        mine, there = slab % Y == y, slab // Y
        by_line = jnp.logical_or(mine, there == Z - 1) if h >= H // 2 else mine
        return functools.reduce(jnp.logical_and, (by_line, there >= z, z > 0))

    def y_ok(slab, h):
        mine, there = slab % Y == y, slab // Y
        if h >= H // 2:
            inner = jnp.logical_and(there > 0, there < Z - 1)
            return jnp.logical_and(mine, jnp.logical_or(slab == c, inner))
        return mine

    def halo_up(slab):
        return jnp.logical_and(low, slab >= c + half)

    def halo_down(slab):
        return jnp.logical_and(jnp.logical_not(low), slab <= c - reach)

    def each(slab, h, act):
        @pl.when(up_ok(slab, h))
        def _():
            act(ag_copy(0, slab, h, c + Y))

        @pl.when(down_ok(slab, h))
        def _():
            act(ag_copy(1, slab, h, c - Y))

        if Y == 2:
            @pl.when(y_ok(slab, h))
            def _():
                act(ag_copy(2, slab, h, z * Y + 1 - y))

        @pl.when(halo_up(slab))
        def _():
            act(halo_copy(slab, slab - half, h, r_up))

        @pl.when(halo_down(slab))
        def _():
            act(halo_copy(slab, slab, h, r_down))

    def start(copy):
        copy.start()

    def receive(slab, h):
        ag_copy(0, slab, h, c).wait_recv()
        each(slab, h, start)

    def use(buf, slab, d, band):
        for n in range(0, NB, 256):
            acc[band, :, n:n + 256] += jnp.dot(ad[d + reach], buf[slab, :, n:n + 256],
                                               preferred_element_type=jnp.float32)

    def use_row(slab):
        d = slab - c

        @pl.when(jnp.logical_and(d <= reach, d >= -reach))
        def _():
            use(rowbuf, slab, d, 0)

    for h in (2, 3, 0, 1):
        each(c, h, start)

    acc[...] = jnp.zeros_like(acc)
    for n in range(NB // 256):
        zrecv[1, n, z] = jnp.zeros(zrecv.shape[3:], jnp.bfloat16)
    copy_a.wait()

    def build(d, carry):
        for i in range(D):
            for s in range(D):
                ad[d, i * B:(i + 1) * B, s * B:(s + 1) * B] = a_scr[i, slots[i, CBR + d * D + s]]
        return carry

    lax.fori_loop(0, 2 * reach + 1, build, 0)
    pt[...] = rowbuf[c].T
    use(rowbuf, c, 0, 0)

    share = NB // C
    width = 256
    parts = NB // width

    def y_copy(band, n):
        return pltpu.make_async_remote_copy(
            src_ref=part16.at[band, n], dst_ref=yrecv.at[band, n], send_sem=y_send.at[band, n],
            recv_sem=y_recv.at[band, n], device_id=dev(r, z * Y + 1 - y), device_id_type=MESH)

    def z_copy(band, n, to, slot):
        return pltpu.make_async_remote_copy(
            src_ref=zsend.at[band, n, to], dst_ref=zrecv.at[band, n, slot], send_sem=z_send.at[band, n, to],
            recv_sem=z_recv.at[band, n, slot], device_id=dev(r, to * Y + y), device_id_type=MESH)

    def partial(band):
        for n in range(parts):
            ap = acc[band, :, n * width:(n + 1) * width].astype(jnp.bfloat16)
            res = jnp.dot(pt[...], ap, preferred_element_type=jnp.float32)
            for t in range(C):
                partf[band, n, t % Y, t // Y] = res[t * share:(t + 1) * share]
            if Y == 2:
                part16[band, n] = partf[band, n, 1 - y].astype(jnp.bfloat16)
                y_copy(band, n).start()

    def spread(band):
        for n in range(parts):
            if Y == 2:
                y_copy(band, n).wait_recv()
            for k in range(1, Z):
                t = lax.rem(z + k, Z)
                total = partf[band, n, y, t]
                if Y == 2:
                    total = total + yrecv[band, n, t].astype(jnp.float32)
                zsend[band, n, t] = total.astype(jnp.bfloat16)
                z_copy(band, n, t, z).start()
            total = partf[band, n, y, z]
            if Y == 2:
                total = total + yrecv[band, n, z].astype(jnp.float32)
            own[band, n] = total

    def line(k, carry):
        pairs = ((z - k, z - k >= 0), (z + k, z + k < Z))
        cross = ((z - k + 1, z - k + 1 >= 0), (z + k - 1, jnp.logical_and(z + k - 1 < Z, k > 1)))
        for h in (2, 3, 0, 1):
            for there, ok in pairs:
                @pl.when(ok)
                def _():
                    receive(there * Y + y, h)
            if Y == 2:
                for there, ok in cross:
                    @pl.when(ok)
                    def _():
                        receive(there * Y + 1 - y, h)
        for there, ok in pairs:
            @pl.when(ok)
            def _():
                use_row(there * Y + y)
        if Y == 2:
            for there, ok in cross:
                @pl.when(ok)
                def _():
                    use_row(there * Y + 1 - y)

        @pl.when(k == Z // 2 + Y - 1)
        def _():
            partial(0)
        return carry

    lax.fori_loop(1, Z + Y - 1, line, 0)

    def halo_use(t, carry):
        idx = jnp.where(low, t, reach - 1 - t)

        @pl.when(jnp.logical_or(jnp.logical_and(low, idx >= c), jnp.logical_and(jnp.logical_not(low), idx <= c - reach)))
        def _():
            for h in range(H):
                halo_copy(c, idx, h, r_up).wait_recv()
            use(halo, idx, jnp.where(low, idx - reach - c, C + idx - c), 1)
        return carry

    lax.fori_loop(0, reach, halo_use, 0)
    partial(1)

    spread(0)
    spread(1)

    def place(band, n, first):
        columns = slice(first + n * width, first + (n + 1) * width)
        total = own[band, n]
        for k in range(1, Z):
            t = lax.rem(z + k, Z)
            z_copy(band, n, t, t).wait_recv()
            total += zrecv[band, n, t].astype(jnp.float32)
        out[:, columns] = total

    def place_sides(n):
        for k in range(1, Z):
            t = lax.rem(z + k, Z)
            z_copy(1, n, t, t).wait_recv()
        mine = own[1, n]
        for side in range(2):
            first = side * 2 * NB + n * width
            total = jnp.where(low == (side == 0), mine, 0.0)
            for t in range(side * (Z // 2), (side + 1) * (Z // 2)):
                total += zrecv[1, n, t].astype(jnp.float32)
            out[:, first:first + width] = total

    for n in range(parts):
        place(0, n, NB)
    for n in range(parts):
        place_sides(n)

    for band in range(2):
        for n in range(parts):
            if Y == 2:
                y_copy(band, n).wait_send()
            for k in range(1, Z):
                z_copy(band, n, lax.rem(z + k, Z), z).wait_send()

    def drain(slab, carry):
        for h in range(H):
            each(slab, h, lambda copy: copy.wait_send())
        return carry

    lax.fori_loop(0, C, drain, 0)


def local(Y, a_tiles, a_cols, p_tiles, p_cols):
    D, KA, B = a_tiles.shape[:3]
    KP = p_tiles.shape[1]
    C, R = lax.axis_size("col"), lax.axis_size("row")
    Z = C // Y
    slab_len = D * C
    total_rows = slab_len * R
    CBR = slab_len // AGG
    NB = CBR * B
    reach = slab_len // 2
    rs = C // 2
    first_row = (lax.axis_index("row") * C + lax.axis_index("col")) * D
    own_cols = lax.dynamic_slice_in_dim(p_cols, first_row, D, 0) % CBR
    m_ids = jnp.arange(CBR, dtype=jnp.int32)
    q_ids = KP - jnp.arange(KP, dtype=jnp.int32)
    p_slot = KP - jnp.max(jnp.where(own_cols[:, :, None] == m_ids, q_ids[:, None], 0), axis=1)
    rel = (a_cols - first_row + reach) % total_rows
    e_ids = jnp.arange(2 * reach + D, dtype=jnp.int32)
    j_ids = KA - jnp.arange(KA, dtype=jnp.int32)
    a_slot = KA - jnp.max(jnp.where(rel[:, :, None] == e_ids, j_ids[:, None], 0), axis=1)
    slots = jnp.concatenate([p_slot, a_slot], axis=1)
    bf, f32 = jnp.bfloat16, jnp.float32
    share = NB // C
    width = 256
    N = NB // width
    S = pltpu.SemaphoreType.DMA
    V = pltpu.VMEM
    return pl.pallas_call(
        functools.partial(kernel, (R, C, Z, Y, D, KA, KP, B, CBR)),
        out_shape=jax.ShapeDtypeStruct((share, 3 * NB), f32),
        in_specs=[pl.BlockSpec(memory_space=pltpu.SMEM), pl.BlockSpec(memory_space=pl.ANY),
                  pl.BlockSpec(memory_space=pl.ANY)],
        out_specs=pl.BlockSpec(memory_space=pltpu.VMEM),
        scratch_shapes=[
            V((D, KA + 1, B, B), bf), V((D, KP + 1, B, B), bf),
            V((2 * rs + 1, D * B, D * B), bf), V((NB, D * B), bf),
            V((C, D * B, NB), bf), V((rs, D * B, NB), bf),
            V((2, D * B, NB), f32), V((2, N, Y, Z, share, width), f32),
            V((2, N, Z, share, width), bf), V((2, N, Z, share, width), bf),
            V((2, N, Z, share, width), bf), V((2, N, share, width), f32), V((2, N, Z, share, width), bf),
            S((2,)), S((3, C, 4)), S((C, 4)), S((rs, 4)), S((rs, 4)), S((2, N)), S((2, N)), S((2, N, Z)), S((2, N, Z)),
        ],
        compiler_params=pltpu.CompilerParams(collective_id=0, has_side_effects=True,
                                             vmem_limit_bytes=60 * 1024 * 1024),
    )(slots, a_tiles, p_tiles)


def solution(mesh):
    Y = 2 if mesh.shape["groups"] == 1 else 1
    in_specs = (
        P(("groups", "row", "col"), None, None, None),
        P(("groups", "row", "col"), None),
        P(("groups", "row", "col"), None, None, None),
        P("groups", None),
    )
    out_specs = P(("groups", "row", "col"), None)
    return jax.shard_map(functools.partial(local, Y), mesh=mesh, in_specs=in_specs, out_specs=out_specs,
                         check_vma=False)
```
